32 devices in a mesh: groups: 2 (over y), ctx: 8 (over z, x), sub: 2 (over core).
Axes of the slice: x: 2, y: 2, z: 4, core: 2. Of those that a mesh axis runs over, the one named last changes fastest.
Arguments:
- queries: bfloat16 [2048, 1024], P(('groups', 'ctx'), 'sub'), parts along dimension 0, may hold values from -6 to 6
- key_vectors: bfloat16 [2048, 128], P(('groups', 'ctx')), parts along dimension 0, may hold values from -6 to 6
- value_vectors: bfloat16 [2048, 128], P(('groups', 'ctx')), parts along dimension 0, may hold values from -6 to 6
- attn_output: bfloat16 [2048, 1024], P(('groups', 'ctx'), 'sub'), parts along dimension 0, may hold values from -6 to 6
- grad_output: bfloat16 [2048, 1024], P(('groups', 'ctx'), 'sub'), parts along dimension 0, may hold values from -4 to 4
- row_logsum: float32 [8, 2048], P('sub', ('groups', 'ctx')), parts along dimension 1, may hold values from -0.5 to 7
- block_place: int32 [16], P('groups'), parts along dimension 0, may hold values from 0 to 7, as said below
Outputs:
- grad_queries: bfloat16 [2048, 1024], P(('groups', 'ctx'), 'sub'), parts along dimension 0
- grad_keys: bfloat16 [2048, 128], P(('groups', 'ctx')), parts along dimension 0
- grad_values: bfloat16 [2048, 128], P(('groups', 'ctx')), parts along dimension 0
The draws below stay inside these ranges and needn't reach their ends.
There are 2 independent parts, one for each index of `groups`. The reference program is written for one: setup_inputs(seed, part) draws one part's arguments, and reference() takes and returns one part's arrays. A program takes and returns all parts, laid end to end along the dimension named above; each array names one. Nothing has to cross between parts.
Inputs may be any that keep to these rules, and one draw needn't show every extreme that they name: `block_place`: a permutation of 0 to 7.
All inputs are finite; a program needn't handle non-finite values.
Results may differ from the reference program's by a relative error of at most 0.0055.
Values may be sent and summed in bfloat16 or wider, within the bound.
A program may use at most 64 MiB of HBM per device.

```python
import math
import jax
import jax.numpy as jnp
from jax import lax

HEAD = 128
HQ = 8
TOK_DEV = 128
SEQ = 1024
NBLK = 8


def shared_order(key):
    return jax.random.permutation(jax.random.fold_in(key, 11), NBLK).astype(jnp.int32)


def draw_block_place(key, part):
    return shared_order(key)


def draw_row_logsum(key, part):
    order = shared_order(key)
    slot_ids = jnp.arange(SEQ, dtype=jnp.int32)
    positions = order[slot_ids // TOK_DEV] * TOK_DEV + slot_ids % TOK_DEV
    base = 0.5 * jnp.log(positions.astype(jnp.float32) + 1.0) + 0.5
    noise_key = jax.random.fold_in(key, 23)
    noise = jax.random.uniform(noise_key, (HQ, SEQ), jnp.float32, -0.4, 0.4)
    return (base[None, :] + noise).astype(jnp.float32)


def shard_levels(stream_key, dims, pieces, smallest, high):
    def one(position, blocks):
        draws = jax.random.uniform(jax.random.fold_in(jax.random.fold_in(stream_key, 6), position), (blocks,), jnp.float32, smallest / len(pieces), high / len(pieces))
        return jnp.repeat(jnp.exp(draws), dims[position] // blocks).reshape((-1,) + (1,) * (len(dims) - position - 1))

    factor_of = one(*pieces[0])
    for cut in pieces[1:]:
        factor_of = factor_of * one(*cut)
    return factor_of


def bell_draw(own_key, shape, spread, bound, pieces=(), kind=jnp.bfloat16):
    entries = jax.random.normal(own_key, shape, jnp.float32) * spread
    if len(pieces) > 0:
        entries = shard_levels(own_key, shape, pieces, -0.22, 0.18) * entries
    return jnp.clip(entries, min=-bound, max=bound).astype(kind)


def setup_inputs(seed: int = 0, part: int = 0) -> dict:
    arg_keys = jax.random.split(jax.random.key(seed), 8)
    part_keys = jax.random.split(jax.random.fold_in(arg_keys[7], part), 8)
    queries = bell_draw(part_keys[0], (SEQ, HQ * HEAD), 1.0, 6.0, ((0, 8), (1, 2)))
    key_vectors = bell_draw(part_keys[1], (SEQ, HEAD), 1.0, 6.0, ((0, 8),))
    value_vectors = bell_draw(part_keys[2], (SEQ, HEAD), 1.0, 6.0, ((0, 8),))
    attn_output = bell_draw(part_keys[3], (SEQ, HQ * HEAD), 1.0, 6.0, ((0, 8), (1, 2)))
    grad_output = bell_draw(part_keys[4], (SEQ, HQ * HEAD), 0.3, 4.0, ((0, 8), (1, 2)))
    row_logsum = draw_row_logsum(jax.random.fold_in(jax.random.fold_in(arg_keys[7], part), 71), part)
    block_place = draw_block_place(jax.random.fold_in(jax.random.fold_in(arg_keys[7], part), 71), part)
    return {"queries": queries, "key_vectors": key_vectors, "value_vectors": value_vectors, "attn_output": attn_output, "grad_output": grad_output, "row_logsum": row_logsum, "block_place": block_place}


def reference(queries, key_vectors, value_vectors, attn_output, grad_output, row_logsum, block_place):
    score_scale = HEAD ** -0.5
    slot_ids = jnp.arange(SEQ, dtype=jnp.int32)
    positions = (block_place[slot_ids // TOK_DEV] * TOK_DEV + slot_ids % TOK_DEV).astype(jnp.int32)
    query_heads = queries.reshape(SEQ, HQ, HEAD)
    grad_heads = grad_output.reshape(SEQ, HQ, HEAD)
    row_delta = jnp.sum(grad_heads.astype(jnp.float32) * attn_output.reshape(SEQ, HQ, HEAD).astype(jnp.float32), axis=2)
    key_wide = key_vectors.astype(jnp.float32)
    value_wide = value_vectors.astype(jnp.float32)
    block_rows = math.gcd(SEQ, 256)
    block_count = SEQ // block_rows

    def one_block(state_pair, block_index):
        key_acc, value_acc = state_pair
        row_start = (block_index * block_rows).astype(jnp.int32)
        query_rows = lax.dynamic_slice_in_dim(query_heads, row_start, block_rows, 0).astype(jnp.float32)
        grad_rows = lax.dynamic_slice_in_dim(grad_heads, row_start, block_rows, 0).astype(jnp.float32)
        lse_rows = lax.dynamic_slice_in_dim(row_logsum, row_start, block_rows, 1).T
        delta_rows = lax.dynamic_slice_in_dim(row_delta, row_start, block_rows, 0)
        place_rows = lax.dynamic_slice_in_dim(positions, row_start, block_rows, 0)
        scores = jnp.einsum("rhd,kd->rhk", query_rows, key_wide) * score_scale
        allowed = positions[None, None, :] <= place_rows[:, None, None]
        attn_prob = jnp.where(allowed, jnp.exp(scores - lse_rows[:, :, None]), 0.0)
        prob_half = lax.optimization_barrier(attn_prob.astype(jnp.bfloat16)).astype(jnp.float32)
        grad_prob = jnp.einsum("rhd,kd->rhk", grad_rows, value_wide)
        grad_score = lax.optimization_barrier((attn_prob * (grad_prob - delta_rows[:, :, None])).astype(jnp.bfloat16)).astype(jnp.float32)
        grad_rows_query = (jnp.einsum("rhk,kd->rhd", grad_score, key_wide) * score_scale).astype(jnp.bfloat16)
        key_acc = key_acc + jnp.einsum("rhk,rhd->kd", grad_score, query_rows)
        value_acc = value_acc + jnp.einsum("rhk,rhd->kd", prob_half, grad_rows)
        return (key_acc, value_acc), grad_rows_query.reshape(block_rows, HQ * HEAD)

    zero_acc = jnp.zeros((SEQ, HEAD), jnp.float32)
    (key_acc, value_acc), query_blocks = lax.scan(one_block, (zero_acc, zero_acc), jnp.arange(block_count, dtype=jnp.int32))
    grad_queries = query_blocks.reshape(SEQ, HQ * HEAD)
    return grad_queries, (key_acc * score_scale).astype(jnp.bfloat16), value_acc.astype(jnp.bfloat16)
```

```python
import functools
import math

import jax
import jax.numpy as jnp
from jax import lax
from jax.experimental import pallas as pl
from jax.experimental.pallas import tpu as pltpu
from jax.sharding import PartitionSpec as P


def partner(value, axis, distance):
    mask = 2**distance
    pairs = [(source, source ^ mask) for source in range(lax.axis_size(axis))]
    return lax.ppermute(value, axis, pairs)


def table_lookup(table, wanted):
    slot_ids = jnp.arange(table.shape[0], dtype=jnp.int32)
    return jnp.sum(jnp.where(wanted[:, None] == slot_ids[None, :], table[None, :], 0), axis=1)


def double_up(pieces, extra):
    return tuple((jnp.concatenate([mine, theirs], axis=0) for mine, theirs in zip(pieces, extra)))


def reduce_keys(key_sum, value_sum, first_bit):
    for section_bit in reversed(range(key_sum.shape[0].bit_length() - 1)):
        halfway = 1 << section_bit
        far_key, far_value = partner(
            (key_sum[halfway:], value_sum[halfway:]), "ctx", first_bit + section_bit
        )
        key_sum = key_sum[:halfway] + far_key
        value_sum = value_sum[:halfway] + far_value
    return (key_sum[0], value_sum[0])


def per_device(
    queries, key_vectors, value_vectors, attn_output, grad_output, row_logsum, block_place
):
    ctx_count = lax.axis_size("ctx")
    bit_count = ctx_count.bit_length() - 1
    row_bits = (bit_count + 1) // 2
    own_index = lax.axis_index("ctx")
    tokens = queries.shape[0]
    head_size = key_vectors.shape[1]
    head_count = row_logsum.shape[0]
    score_scale = head_size ** (-0.5)
    row_delta = jnp.einsum(
        "thd,thd->ht",
        grad_output.reshape(tokens, head_count, head_size),
        attn_output.reshape(tokens, head_count, head_size),
        preferred_element_type=jnp.float32,
    )
    row_query, row_grad = (queries[None], grad_output[None])
    row_lse_all, row_delta_all = (row_logsum[None], row_delta[None])
    for section_bit in range(row_bits):
        far_query, far_grad = partner((row_query, row_grad), "ctx", section_bit)
        far_lse, far_delta = partner((row_lse_all, row_delta_all), "ctx", section_bit)
        row_query, row_grad = double_up((row_query, row_grad), (far_query, far_grad))
        row_lse_all, row_delta_all = double_up((row_lse_all, row_delta_all), (far_lse, far_delta))
    col_key, col_value = (key_vectors[None], value_vectors[None])
    for section_bit in range(row_bits, bit_count):
        far_key, far_value = partner((col_key, col_value), "ctx", section_bit)
        col_key, col_value = double_up((col_key, col_value), (far_key, far_value))
    row_total = 1 << row_bits
    col_total = 1 << bit_count - row_bits
    pair_width = min(2, col_total)
    group_count = col_total // pair_width
    group_rows = pair_width * tokens
    row_blocks = table_lookup(
        block_place, jnp.bitwise_xor(own_index, jnp.arange(row_total, dtype=jnp.int32))
    )
    col_blocks = table_lookup(
        block_place, jnp.bitwise_xor(own_index, jnp.arange(col_total, dtype=jnp.int32) * row_total)
    )
    offsets = jnp.arange(tokens, dtype=jnp.int32)
    group_place = (col_blocks[:, None] * tokens + offsets[None, :]).reshape(group_count, group_rows)
    group_first = jnp.min(col_blocks.reshape(group_count, pair_width), axis=1)
    key_groups = col_key.reshape(group_count, group_rows, head_size)
    value_groups = col_value.reshape(group_count, group_rows, head_size)
    row_tiles = row_query.reshape(row_total, tokens, head_count, head_size)
    grad_tiles = row_grad.reshape(row_total, tokens, head_count, head_size)

    def row_sweep(key_state, row_index):
        query_tile = row_tiles[row_index]
        grad_tile = grad_tiles[row_index]
        lse_tile = row_lse_all[row_index].T
        delta_tile = row_delta_all[row_index].T
        row_block = row_blocks[row_index]
        row_place = row_block * tokens + offsets

        def group_sweep(tile_state, group_index):

            def visible(state):
                query_acc, key_acc, value_acc = state
                key_tile = key_groups[group_index]
                value_tile = value_groups[group_index]
                col_place = group_place[group_index]
                scores = (
                    jnp.einsum(
                        "thd,kd->thk", query_tile, key_tile, preferred_element_type=jnp.float32
                    )
                    * score_scale
                )
                allowed = col_place[None, None, :] <= row_place[:, None, None]
                attn_prob = jnp.where(allowed, jnp.exp(scores - lse_tile[:, :, None]), 0.0)
                prob_half = attn_prob.astype(jnp.bfloat16)
                grad_prob = jnp.einsum(
                    "thd,kd->thk", grad_tile, value_tile, preferred_element_type=jnp.float32
                )
                grad_score = (attn_prob * (grad_prob - delta_tile[:, :, None])).astype(jnp.bfloat16)
                query_acc = query_acc + jnp.einsum(
                    "thk,kd->thd", grad_score, key_tile, preferred_element_type=jnp.float32
                )
                key_term = jnp.einsum(
                    "thk,thd->kd", grad_score, query_tile, preferred_element_type=jnp.float32
                )
                value_term = jnp.einsum(
                    "thk,thd->kd", prob_half, grad_tile, preferred_element_type=jnp.float32
                )
                key_acc = key_acc.at[group_index].add(key_term)
                value_acc = value_acc.at[group_index].add(value_term)
                return (query_acc, key_acc, value_acc)

            tile_state = lax.cond(
                group_first[group_index] <= row_block, visible, lambda state: state, tile_state
            )
            return (tile_state, None)

        query_zero = jnp.zeros((tokens, head_count, head_size), jnp.float32)
        start_state = (query_zero, key_state[0], key_state[1])
        (query_acc, key_acc, value_acc), unused = lax.scan(
            group_sweep, start_state, jnp.arange(group_count, dtype=jnp.int32)
        )
        return ((key_acc, value_acc), query_acc)

    kv_zero = jnp.zeros((group_count, group_rows, head_size), jnp.float32)
    (key_grouped, value_grouped), query_terms = lax.scan(
        row_sweep, (kv_zero, kv_zero), jnp.arange(row_total, dtype=jnp.int32)
    )
    key_total = key_grouped.reshape(col_total, tokens, head_size)
    value_total = value_grouped.reshape(col_total, tokens, head_size)
    query_sum = query_terms
    for section_bit in reversed(range(row_bits)):
        halfway = 1 << section_bit
        query_sum = query_sum[:halfway] + partner(query_sum[halfway:], "ctx", section_bit)
    grad_queries = (
        (query_sum[0] * score_scale).reshape(tokens, head_count * head_size).astype(jnp.bfloat16)
    )
    key_sum, value_sum = reduce_keys(key_total, value_total, row_bits)
    key_sum, value_sum = lax.psum((key_sum, value_sum), "sub")
    grad_keys = (key_sum * score_scale).astype(jnp.bfloat16)
    grad_values = value_sum.astype(jnp.bfloat16)
    return (grad_queries, grad_keys, grad_values)


MOST_BLOCKS = 16
MESH = pl.DeviceIdType.MESH
HIDE = 1e30


def fused_kernel(
    n, heads,
    q_hbm, k_hbm, v_hbm, o_hbm, g_hbm, l_hbm, place,
    dq_hbm, dk_hbm, dv_hbm,
    q_v, o_v, g_v, l_v, kv, qt, gt, qs, gs, ds_all, part, sub_in,
    x_out, x_in, z_out, z_in, fin, dq_v,
    load_sem, kz_send, kz_recv, kx_send, kx_recv, ks_send, ks_recv,
    ps_send, ps_recv, px_send, px_recv, pz_send, pz_recv, fin_sem, out_sem,
):
    nz = n // 2
    tokens, size = k_hbm.shape
    width = heads * tokens
    scale = size ** (-0.5)
    log2e = math.log2(math.e)
    g = lax.axis_index("groups")
    t = lax.axis_index("ctx")
    s = lax.axis_index("sub")
    z, x = t // 2, t % 2
    far = [((z + e) % nz) * 2 + x for e in range(nz)]
    side = [((z + e) % nz) * 2 + (1 - x) for e in range(nz)]

    loads = [
        pltpu.make_async_copy(k_hbm, kv.at[0, 0], load_sem.at[0]),
        pltpu.make_async_copy(v_hbm, kv.at[0, 1], load_sem.at[1]),
        pltpu.make_async_copy(q_hbm, q_v, load_sem.at[2]),
        pltpu.make_async_copy(g_hbm, g_v, load_sem.at[3]),
        pltpu.make_async_copy(o_hbm, o_v, load_sem.at[4]),
        pltpu.make_async_copy(l_hbm, l_v, load_sem.at[5]),
    ]
    for load in loads:
        load.start()

    peers = [(g, far[e], s) for e in range(1, nz)] + [(g, side[0], s), (g, t, 1 - s)]
    barrier = pltpu.get_barrier_semaphore()
    for peer in peers:
        pl.semaphore_signal(barrier, inc=1, device_id=peer, device_id_type=MESH)
    loads[0].wait()
    loads[1].wait()
    pl.semaphore_wait(barrier, len(peers))

    def send(source, target, send_sem, recv_sem, device):
        copy = pltpu.make_async_remote_copy(
            src_ref=source, dst_ref=target, send_sem=send_sem, recv_sem=recv_sem,
            device_id=device, device_id_type=MESH,
        )
        copy.start()
        return copy

    sent = []
    kz, kx, ks = {}, {}, {}
    row_order = list(range(1, nz))
    for e in sorted(row_order, key=lambda e: -min(e, nz - e)):
        kz[nz - e] = send(
            kv.at[0, s], kv.at[2 * (nz - e), s], kz_send.at[e], kz_recv.at[nz - e], (g, far[e], s)
        )
    kx[0] = send(kv.at[0, s], kv.at[1, s], kx_send.at[0], kx_recv.at[0], (g, side[0], s))

    for load in loads[2:]:
        load.wait()
    deltas = []
    for h in range(heads):
        here = slice(h * tokens, (h + 1) * tokens)
        cols = slice(h * size, (h + 1) * size)
        qs[here, :] = q_v[:, cols]
        gs[here, :] = g_v[:, cols]
        qt[:, here] = q_v[:, cols].T
        grad_t = g_v[:, cols].T
        gt[:, here] = grad_t
        out_t = o_v[:, cols].T
        deltas.append(
            jnp.sum(grad_t.astype(jnp.float32) * out_t.astype(jnp.float32), axis=0, keepdims=True)
        )
    delta_row = jnp.concatenate(deltas, axis=1)
    lse_row = jnp.concatenate([l_v[h : h + 1, :] for h in range(heads)], axis=1) * log2e

    own_place = place[t]
    chunk = 2 * tokens if heads % 2 == 0 else tokens

    def score(slot):
        key_tile, value_tile = kv[slot, 0], kv[slot, 1]
        lse = lse_row
        if slot:
            there = side[slot // 2] if slot % 2 else far[slot // 2]
            lse = lse + jnp.where(place[there] < own_place, 0.0, HIDE)
        key_sum = value_sum = None
        for start in range(0, width, chunk):
            here = slice(start, start + chunk)
            scores = jnp.dot(key_tile, qt[:, here], preferred_element_type=jnp.float32)
            grad_prob = jnp.dot(value_tile, gt[:, here], preferred_element_type=jnp.float32)
            prob = jnp.exp2(scores * (scale * log2e) - lse[:, here])
            if slot == 0:
                shape = (tokens, chunk)
                key_place = lax.broadcasted_iota(jnp.int32, shape, 0)
                row_place = lax.broadcasted_iota(jnp.int32, shape, 1) % tokens
                prob = jnp.where(key_place <= row_place, prob, 0.0)
            grad_score = (prob * (grad_prob - delta_row[:, here])).astype(jnp.bfloat16)
            ds_all[slot, :, here] = grad_score
            value_term = jnp.dot(
                prob.astype(jnp.bfloat16), gs[here, :], preferred_element_type=jnp.float32
            )
            key_term = jnp.dot(grad_score, qs[here, :], preferred_element_type=jnp.float32)
            value_sum = value_term if value_sum is None else value_sum + value_term
            key_sum = key_term if key_sum is None else key_sum + key_term
        part[slot, 0] = key_sum
        part[slot, 1] = value_sum
        sent_part[slot] = send(
            part.at[slot, 1 - s], sub_in.at[slot], ps_send.at[slot], ps_recv.at[slot],
            (g, t, 1 - s),
        )

    sent_part = {}
    px, pz = {}, {}

    def pass_on(slot):
        sent_part[slot].wait_recv()
        total = part[slot, s] + sub_in[slot]
        e = slot // 2
        if slot % 2:
            x_out[e] = total.astype(jnp.bfloat16)
            px[e] = send(x_out.at[e], x_in.at[e], px_send.at[e], px_recv.at[e], (g, side[0], s))
        else:
            part[slot, s] = total

    def share(slot):
        ks[slot] = send(
            kv.at[slot, s], kv.at[slot, s], ks_send.at[slot], ks_recv.at[slot], (g, t, 1 - s)
        )

    score(0)
    near_first = sorted(row_order, key=lambda e: min(e, nz - e))
    for e in near_first:
        kz[e].wait_recv()
        kx[e] = send(
            kv.at[2 * e, s], kv.at[2 * e + 1, s], kx_send.at[e], kx_recv.at[e], (g, side[0], s)
        )
        share(2 * e)
    kx[0].wait_recv()
    share(1)
    order = [1] + [2 * e for e in near_first] + [2 * e + 1 for e in near_first]
    before = 0
    waiting = list(near_first)
    for place_in_order, slot in enumerate(order):
        ks[slot].wait_recv()
        score(slot)
        pass_on(before)
        before = slot
        if place_in_order >= 1 and waiting:
            e = waiting.pop(0)
            kx[e].wait_recv()
            share(2 * e + 1)
    pass_on(before)

    for e in near_first:
        px[e].wait_recv()
        z_out[e] = (part[2 * e, s] + x_in[e].astype(jnp.float32)).astype(jnp.bfloat16)
        pz[nz - e] = send(
            z_out.at[e], z_in.at[nz - e], pz_send.at[e], pz_recv.at[nz - e], (g, far[e], s)
        )
    px[0].wait_recv()
    total = part[0, s] + x_in[0].astype(jnp.float32)

    keys = kv[:, 0].reshape(n * tokens, size)
    for start in range(0, width, chunk):
        grads = ds_all[:, :, start : start + chunk].reshape(n * tokens, chunk)
        query_t = lax.dot_general(
            keys, grads, (((0,), (0,)), ((), ())), preferred_element_type=jnp.float32
        )
        for first in range(0, chunk, tokens):
            h = (start + first) // tokens
            dq_v[:, h * size : (h + 1) * size] = (
                (query_t[:, first : first + tokens] * scale).T.astype(jnp.bfloat16)
            )
    outs = [pltpu.make_async_copy(dq_v, dq_hbm, out_sem.at[0])]
    outs[0].start()

    for e in near_first:
        pz[e].wait_recv()
        total = total + z_in[e].astype(jnp.float32)
    fin[s] = (total * jnp.where(s == 0, scale, 1.0)).astype(jnp.bfloat16)
    last = send(fin.at[s], fin.at[s], fin_sem.at[0], fin_sem.at[1], (g, t, 1 - s))
    last.wait_recv()
    outs.append(pltpu.make_async_copy(fin.at[0], dk_hbm, out_sem.at[1]))
    outs.append(pltpu.make_async_copy(fin.at[1], dv_hbm, out_sem.at[2]))
    outs[1].start()
    outs[2].start()
    for group in (kz, kx, ks, sent_part, px, pz):
        for copy in group.values():
            copy.wait_send()
    last.wait_send()
    for out in outs:
        out.wait()


def fused_device(
    queries, key_vectors, value_vectors, attn_output, grad_output, row_logsum, block_place
):
    n = lax.axis_size("ctx")
    nz = n // 2
    tokens, size = key_vectors.shape
    heads = row_logsum.shape[0]
    width = heads * tokens
    half, wide = jnp.bfloat16, jnp.float32
    dma = pltpu.SemaphoreType.DMA
    anywhere = pl.BlockSpec(memory_space=pl.ANY)
    return pl.pallas_call(
        functools.partial(fused_kernel, n, heads),
        out_shape=(
            jax.ShapeDtypeStruct(queries.shape, half),
            jax.ShapeDtypeStruct(key_vectors.shape, half),
            jax.ShapeDtypeStruct(value_vectors.shape, half),
        ),
        in_specs=[anywhere] * 6 + [pl.BlockSpec(memory_space=pltpu.SMEM)],
        out_specs=(anywhere,) * 3,
        scratch_shapes=[
            pltpu.VMEM(queries.shape, half),
            pltpu.VMEM(queries.shape, half),
            pltpu.VMEM(queries.shape, half),
            pltpu.VMEM(row_logsum.shape, wide),
            pltpu.VMEM((n, 2, tokens, size), half),
            pltpu.VMEM((size, width), half),
            pltpu.VMEM((size, width), half),
            pltpu.VMEM((width, size), half),
            pltpu.VMEM((width, size), half),
            pltpu.VMEM((n, tokens, width), half),
            pltpu.VMEM((n, 2, tokens, size), wide),
            pltpu.VMEM((n, tokens, size), wide),
            pltpu.VMEM((nz, tokens, size), half),
            pltpu.VMEM((nz, tokens, size), half),
            pltpu.VMEM((nz, tokens, size), half),
            pltpu.VMEM((nz, tokens, size), half),
            pltpu.VMEM((2, tokens, size), half),
            pltpu.VMEM(queries.shape, half),
            dma((6,)),
            dma((nz,)), dma((nz,)),
            dma((nz,)), dma((nz,)),
            dma((n,)), dma((n,)),
            dma((n,)), dma((n,)),
            dma((nz,)), dma((nz,)),
            dma((nz,)), dma((nz,)),
            dma((2,)),
            dma((3,)),
        ],
        compiler_params=pltpu.CompilerParams(
            collective_id=0, has_side_effects=True, vmem_limit_bytes=32 * 2**20
        ),
        cost_estimate=pl.CostEstimate(
            flops=10 * n * tokens * width * size,
            bytes_accessed=8 * tokens * width,
            transcendentals=n * tokens * width,
        ),
    )(queries, key_vectors, value_vectors, attn_output, grad_output, row_logsum, block_place)


def solution(mesh):
    placed = (
        P(("groups", "ctx"), "sub"),
        P(("groups", "ctx"), None),
        P(("groups", "ctx"), None),
        P(("groups", "ctx"), "sub"),
        P(("groups", "ctx"), "sub"),
        P("sub", ("groups", "ctx")),
        P("groups"),
    )
    ctx_count = mesh.shape["ctx"]
    fused = ctx_count % 2 == 0 and 4 <= ctx_count <= MOST_BLOCKS and mesh.shape["sub"] == 2
    return jax.shard_map(
        fused_device if fused else per_device,
        mesh=mesh,
        in_specs=placed,
        out_specs=(
            P(("groups", "ctx"), "sub"),
            P(("groups", "ctx"), None),
            P(("groups", "ctx"), None),
        ),
        check_vma=False,
    )
```

```python
import functools
import math

import jax
import jax.numpy as jnp
from jax import lax
from jax.experimental import pallas as pl
from jax.experimental.pallas import tpu as pltpu
from jax.sharding import PartitionSpec as P


def partner(value, axis, distance):
    mask = 2**distance
    pairs = [(source, source ^ mask) for source in range(lax.axis_size(axis))]
    return lax.ppermute(value, axis, pairs)


def table_lookup(table, wanted):
    slot_ids = jnp.arange(table.shape[0], dtype=jnp.int32)
    return jnp.sum(jnp.where(wanted[:, None] == slot_ids[None, :], table[None, :], 0), axis=1)


def double_up(pieces, extra):
    return tuple((jnp.concatenate([mine, theirs], axis=0) for mine, theirs in zip(pieces, extra)))


def reduce_keys(key_sum, value_sum, first_bit):
    for section_bit in reversed(range(key_sum.shape[0].bit_length() - 1)):
        halfway = 1 << section_bit
        far_key, far_value = partner(
            (key_sum[halfway:], value_sum[halfway:]), "ctx", first_bit + section_bit
        )
        key_sum = key_sum[:halfway] + far_key
        value_sum = value_sum[:halfway] + far_value
    return (key_sum[0], value_sum[0])


def per_device(
    queries, key_vectors, value_vectors, attn_output, grad_output, row_logsum, block_place
):
    ctx_count = lax.axis_size("ctx")
    bit_count = ctx_count.bit_length() - 1
    row_bits = (bit_count + 1) // 2
    own_index = lax.axis_index("ctx")
    tokens = queries.shape[0]
    head_size = key_vectors.shape[1]
    head_count = row_logsum.shape[0]
    score_scale = head_size ** (-0.5)
    row_delta = jnp.einsum(
        "thd,thd->ht",
        grad_output.reshape(tokens, head_count, head_size),
        attn_output.reshape(tokens, head_count, head_size),
        preferred_element_type=jnp.float32,
    )
    row_query, row_grad = (queries[None], grad_output[None])
    row_lse_all, row_delta_all = (row_logsum[None], row_delta[None])
    for section_bit in range(row_bits):
        far_query, far_grad = partner((row_query, row_grad), "ctx", section_bit)
        far_lse, far_delta = partner((row_lse_all, row_delta_all), "ctx", section_bit)
        row_query, row_grad = double_up((row_query, row_grad), (far_query, far_grad))
        row_lse_all, row_delta_all = double_up((row_lse_all, row_delta_all), (far_lse, far_delta))
    col_key, col_value = (key_vectors[None], value_vectors[None])
    for section_bit in range(row_bits, bit_count):
        far_key, far_value = partner((col_key, col_value), "ctx", section_bit)
        col_key, col_value = double_up((col_key, col_value), (far_key, far_value))
    row_total = 1 << row_bits
    col_total = 1 << bit_count - row_bits
    pair_width = min(2, col_total)
    group_count = col_total // pair_width
    group_rows = pair_width * tokens
    row_blocks = table_lookup(
        block_place, jnp.bitwise_xor(own_index, jnp.arange(row_total, dtype=jnp.int32))
    )
    col_blocks = table_lookup(
        block_place, jnp.bitwise_xor(own_index, jnp.arange(col_total, dtype=jnp.int32) * row_total)
    )
    offsets = jnp.arange(tokens, dtype=jnp.int32)
    group_place = (col_blocks[:, None] * tokens + offsets[None, :]).reshape(group_count, group_rows)
    group_first = jnp.min(col_blocks.reshape(group_count, pair_width), axis=1)
    key_groups = col_key.reshape(group_count, group_rows, head_size)
    value_groups = col_value.reshape(group_count, group_rows, head_size)
    row_tiles = row_query.reshape(row_total, tokens, head_count, head_size)
    grad_tiles = row_grad.reshape(row_total, tokens, head_count, head_size)

    def row_sweep(key_state, row_index):
        query_tile = row_tiles[row_index]
        grad_tile = grad_tiles[row_index]
        lse_tile = row_lse_all[row_index].T
        delta_tile = row_delta_all[row_index].T
        row_block = row_blocks[row_index]
        row_place = row_block * tokens + offsets

        def group_sweep(tile_state, group_index):

            def visible(state):
                query_acc, key_acc, value_acc = state
                key_tile = key_groups[group_index]
                value_tile = value_groups[group_index]
                col_place = group_place[group_index]
                scores = (
                    jnp.einsum(
                        "thd,kd->thk", query_tile, key_tile, preferred_element_type=jnp.float32
                    )
                    * score_scale
                )
                allowed = col_place[None, None, :] <= row_place[:, None, None]
                attn_prob = jnp.where(allowed, jnp.exp(scores - lse_tile[:, :, None]), 0.0)
                prob_half = attn_prob.astype(jnp.bfloat16)
                grad_prob = jnp.einsum(
                    "thd,kd->thk", grad_tile, value_tile, preferred_element_type=jnp.float32
                )
                grad_score = (attn_prob * (grad_prob - delta_tile[:, :, None])).astype(jnp.bfloat16)
                query_acc = query_acc + jnp.einsum(
                    "thk,kd->thd", grad_score, key_tile, preferred_element_type=jnp.float32
                )
                key_term = jnp.einsum(
                    "thk,thd->kd", grad_score, query_tile, preferred_element_type=jnp.float32
                )
                value_term = jnp.einsum(
                    "thk,thd->kd", prob_half, grad_tile, preferred_element_type=jnp.float32
                )
                key_acc = key_acc.at[group_index].add(key_term)
                value_acc = value_acc.at[group_index].add(value_term)
                return (query_acc, key_acc, value_acc)

            tile_state = lax.cond(
                group_first[group_index] <= row_block, visible, lambda state: state, tile_state
            )
            return (tile_state, None)

        query_zero = jnp.zeros((tokens, head_count, head_size), jnp.float32)
        start_state = (query_zero, key_state[0], key_state[1])
        (query_acc, key_acc, value_acc), unused = lax.scan(
            group_sweep, start_state, jnp.arange(group_count, dtype=jnp.int32)
        )
        return ((key_acc, value_acc), query_acc)

    kv_zero = jnp.zeros((group_count, group_rows, head_size), jnp.float32)
    (key_grouped, value_grouped), query_terms = lax.scan(
        row_sweep, (kv_zero, kv_zero), jnp.arange(row_total, dtype=jnp.int32)
    )
    key_total = key_grouped.reshape(col_total, tokens, head_size)
    value_total = value_grouped.reshape(col_total, tokens, head_size)
    query_sum = query_terms
    for section_bit in reversed(range(row_bits)):
        halfway = 1 << section_bit
        query_sum = query_sum[:halfway] + partner(query_sum[halfway:], "ctx", section_bit)
    grad_queries = (
        (query_sum[0] * score_scale).reshape(tokens, head_count * head_size).astype(jnp.bfloat16)
    )
    key_sum, value_sum = reduce_keys(key_total, value_total, row_bits)
    key_sum, value_sum = lax.psum((key_sum, value_sum), "sub")
    grad_keys = (key_sum * score_scale).astype(jnp.bfloat16)
    grad_values = value_sum.astype(jnp.bfloat16)
    return (grad_queries, grad_keys, grad_values)


MOST_BLOCKS = 16
MESH = pl.DeviceIdType.MESH
HIDE = 1e30


def fused_kernel(
    n, heads,
    q_hbm, k_hbm, v_hbm, o_hbm, g_hbm, l_hbm, b_hbm,
    dq_hbm, dk_hbm, dv_hbm,
    q_v, o_v, g_v, l_v, kv, qt, gt, qs, gs, ds_all, part, sub_in,
    term_out, term_in, fin, dq_v,
    place, load_sem, kv_send, kv_recv, ks_send, ks_recv,
    ps_send, ps_recv, pt_send, pt_recv, fin_sem, out_sem,
):
    nz = n // 2
    tokens, size = k_hbm.shape
    width = heads * tokens
    scale = size ** (-0.5)
    log2e = math.log2(math.e)
    g = lax.axis_index("groups")
    t = lax.axis_index("ctx")
    s = lax.axis_index("sub")
    z, x = t // 2, t % 2
    block = [((z + i // 2) % nz) * 2 + (x + i % 2) % 2 for i in range(n)]
    mirror = [(nz - i // 2) % nz * 2 + i % 2 for i in range(n)]
    near_first = sorted(range(1, n), key=lambda i: (min(i // 2, nz - i // 2), i % 2))

    loads = [
        pltpu.make_async_copy(k_hbm, kv.at[0, 0], load_sem.at[0]),
        pltpu.make_async_copy(v_hbm, kv.at[0, 1], load_sem.at[1]),
        pltpu.make_async_copy(q_hbm, q_v, load_sem.at[2]),
        pltpu.make_async_copy(g_hbm, g_v, load_sem.at[3]),
        pltpu.make_async_copy(o_hbm, o_v, load_sem.at[4]),
        pltpu.make_async_copy(l_hbm, l_v, load_sem.at[5]),
        pltpu.make_async_copy(b_hbm, place, load_sem.at[6]),
    ]
    for load in loads:
        load.start()

    peers = [(g, block[i], s) for i in range(1, n)] + [(g, t, 1 - s)]
    barrier = pltpu.get_barrier_semaphore()
    for peer in peers:
        pl.semaphore_signal(barrier, inc=1, device_id=peer, device_id_type=MESH)
    loads[0].wait()
    loads[1].wait()
    pl.semaphore_wait(barrier, len(peers))

    def send(source, target, send_sem, recv_sem, device):
        copy = pltpu.make_async_remote_copy(
            src_ref=source, dst_ref=target, send_sem=send_sem, recv_sem=recv_sem,
            device_id=device, device_id_type=MESH,
        )
        copy.start()
        return copy

    came, shared, sent_part, passed = {}, {}, {}, {}
    for i in near_first:
        came[mirror[i]] = send(
            kv.at[0, s], kv.at[mirror[i], s], kv_send.at[i], kv_recv.at[mirror[i]], (g, block[i], s)
        )

    for load in loads[2:]:
        load.wait()
    deltas = []
    for h in range(heads):
        here = slice(h * tokens, (h + 1) * tokens)
        cols = slice(h * size, (h + 1) * size)
        qs[here, :] = q_v[:, cols]
        gs[here, :] = g_v[:, cols]
        qt[:, here] = q_v[:, cols].T
        grad_t = g_v[:, cols].T
        gt[:, here] = grad_t
        out_t = o_v[:, cols].T
        deltas.append(
            jnp.sum(grad_t.astype(jnp.float32) * out_t.astype(jnp.float32), axis=0, keepdims=True)
        )
    delta_row = jnp.concatenate(deltas, axis=1)
    lse_row = jnp.concatenate([l_v[h : h + 1, :] for h in range(heads)], axis=1) * log2e

    own_place = place[t]
    chunk = 2 * tokens if heads % 2 == 0 else tokens

    def score(slot):
        key_tile, value_tile = kv[slot, 0], kv[slot, 1]
        lse = lse_row
        if slot:
            lse = lse + jnp.where(place[block[slot]] < own_place, 0.0, HIDE)
        key_sum = value_sum = None
        for start in range(0, width, chunk):
            here = slice(start, start + chunk)
            scores = jnp.dot(key_tile, qt[:, here], preferred_element_type=jnp.float32)
            grad_prob = jnp.dot(value_tile, gt[:, here], preferred_element_type=jnp.float32)
            prob = jnp.exp2(scores * (scale * log2e) - lse[:, here])
            if slot == 0:
                shape = (tokens, chunk)
                key_place = lax.broadcasted_iota(jnp.int32, shape, 0)
                row_place = lax.broadcasted_iota(jnp.int32, shape, 1) % tokens
                prob = jnp.where(key_place <= row_place, prob, 0.0)
            grad_score = (prob * (grad_prob - delta_row[:, here])).astype(jnp.bfloat16)
            ds_all[slot, :, here] = grad_score
            value_term = jnp.dot(
                prob.astype(jnp.bfloat16), gs[here, :], preferred_element_type=jnp.float32
            )
            key_term = jnp.dot(grad_score, qs[here, :], preferred_element_type=jnp.float32)
            value_sum = value_term if value_sum is None else value_sum + value_term
            key_sum = key_term if key_sum is None else key_sum + key_term
        part[slot, 0] = key_sum
        part[slot, 1] = value_sum
        sent_part[slot] = send(
            part.at[slot, 1 - s], sub_in.at[slot], ps_send.at[slot], ps_recv.at[slot],
            (g, t, 1 - s),
        )

    def pass_on(slot):
        sent_part[slot].wait_recv()
        total = part[slot, s] + sub_in[slot]
        if slot == 0:
            part[slot, s] = total
            return
        term_out[slot] = total.astype(jnp.bfloat16)
        passed[mirror[slot]] = send(
            term_out.at[slot], term_in.at[mirror[slot]], pt_send.at[slot],
            pt_recv.at[mirror[slot]], (g, block[slot], s),
        )

    def share(slot):
        came[slot].wait_recv()
        shared[slot] = send(
            kv.at[slot, s], kv.at[slot, s], ks_send.at[slot], ks_recv.at[slot], (g, t, 1 - s)
        )

    score(0)
    share(near_first[0])
    before = 0
    for i, slot in enumerate(near_first):
        if i + 1 < len(near_first):
            share(near_first[i + 1])
        shared[slot].wait_recv()
        score(slot)
        pass_on(before)
        before = slot
    pass_on(before)
    total = part[0, s]

    keys = kv[:, 0].reshape(n * tokens, size)
    for start in range(0, width, chunk):
        grads = ds_all[:, :, start : start + chunk].reshape(n * tokens, chunk)
        query_t = lax.dot_general(
            keys, grads, (((0,), (0,)), ((), ())), preferred_element_type=jnp.float32
        )
        for first in range(0, chunk, tokens):
            h = (start + first) // tokens
            dq_v[:, h * size : (h + 1) * size] = (
                (query_t[:, first : first + tokens] * scale).T.astype(jnp.bfloat16)
            )
    outs = [pltpu.make_async_copy(dq_v, dq_hbm, out_sem.at[0])]
    outs[0].start()

    for slot in near_first:
        passed[slot].wait_recv()
        total = total + term_in[slot].astype(jnp.float32)
    fin[s] = (total * jnp.where(s == 0, scale, 1.0)).astype(jnp.bfloat16)
    last = send(fin.at[s], fin.at[s], fin_sem.at[0], fin_sem.at[1], (g, t, 1 - s))
    last.wait_recv()
    outs.append(pltpu.make_async_copy(fin.at[0], dk_hbm, out_sem.at[1]))
    outs.append(pltpu.make_async_copy(fin.at[1], dv_hbm, out_sem.at[2]))
    outs[1].start()
    outs[2].start()
    for group in (came, shared, sent_part, passed):
        for copy in group.values():
            copy.wait_send()
    last.wait_send()
    for out in outs:
        out.wait()


def settle_kernel(dq_in, dk_in, dv_in, dq_out, dk_out, dv_out):
    dq_out[...] = dq_in[...]
    dk_out[...] = dk_in[...]
    dv_out[...] = dv_in[...]


def fused_device(
    queries, key_vectors, value_vectors, attn_output, grad_output, row_logsum, block_place
):
    n = lax.axis_size("ctx")
    tokens, size = key_vectors.shape
    heads = row_logsum.shape[0]
    width = heads * tokens
    half, wide = jnp.bfloat16, jnp.float32
    dma = pltpu.SemaphoreType.DMA
    anywhere = pl.BlockSpec(memory_space=pltpu.HBM)
    grads = pl.pallas_call(
        functools.partial(fused_kernel, n, heads),
        out_shape=(
            jax.ShapeDtypeStruct(queries.shape, half),
            jax.ShapeDtypeStruct(key_vectors.shape, half),
            jax.ShapeDtypeStruct(value_vectors.shape, half),
        ),
        in_specs=[anywhere] * 7,
        out_specs=(anywhere,) * 3,
        scratch_shapes=[
            pltpu.VMEM(queries.shape, half),
            pltpu.VMEM(queries.shape, half),
            pltpu.VMEM(queries.shape, half),
            pltpu.VMEM(row_logsum.shape, wide),
            pltpu.VMEM((n, 2, tokens, size), half),
            pltpu.VMEM((size, width), half),
            pltpu.VMEM((size, width), half),
            pltpu.VMEM((width, size), half),
            pltpu.VMEM((width, size), half),
            pltpu.VMEM((n, tokens, width), half),
            pltpu.VMEM((n, 2, tokens, size), wide),
            pltpu.VMEM((n, tokens, size), wide),
            pltpu.VMEM((n, tokens, size), half),
            pltpu.VMEM((n, tokens, size), half),
            pltpu.VMEM((2, tokens, size), half),
            pltpu.VMEM(queries.shape, half),
            pltpu.SMEM(block_place.shape, jnp.int32),
            dma((7,)),
            dma((n,)), dma((n,)),
            dma((n,)), dma((n,)),
            dma((n,)), dma((n,)),
            dma((n,)), dma((n,)),
            dma((2,)),
            dma((3,)),
        ],
        compiler_params=pltpu.CompilerParams(
            collective_id=0, has_side_effects=True, vmem_limit_bytes=60 * 2**20
        ),
        cost_estimate=pl.CostEstimate(
            flops=10 * n * tokens * width * size,
            bytes_accessed=8 * tokens * width,
            transcendentals=n * tokens * width,
        ),
    )(queries, key_vectors, value_vectors, attn_output, grad_output, row_logsum, block_place)
    return pl.pallas_call(
        settle_kernel,
        out_shape=tuple(jax.ShapeDtypeStruct(grad.shape, grad.dtype) for grad in grads),
    )(*grads)


def solution(mesh):
    placed = (
        P(("groups", "ctx"), "sub"),
        P(("groups", "ctx"), None),
        P(("groups", "ctx"), None),
        P(("groups", "ctx"), "sub"),
        P(("groups", "ctx"), "sub"),
        P("sub", ("groups", "ctx")),
        P("groups"),
    )
    ctx_count = mesh.shape["ctx"]
    fused = ctx_count % 2 == 0 and 4 <= ctx_count <= MOST_BLOCKS and mesh.shape["sub"] == 2
    return jax.shard_map(
        fused_device if fused else per_device,
        mesh=mesh,
        in_specs=placed,
        out_specs=(
            P(("groups", "ctx"), "sub"),
            P(("groups", "ctx"), None),
            P(("groups", "ctx"), None),
        ),
        check_vma=False,
    )
```

```python
import functools
import math

import jax
import jax.numpy as jnp
from jax import lax
from jax.experimental import pallas as pl
from jax.experimental.pallas import tpu as pltpu
from jax.sharding import PartitionSpec as P


def partner(value, axis, distance):
    mask = 2**distance
    pairs = [(source, source ^ mask) for source in range(lax.axis_size(axis))]
    return lax.ppermute(value, axis, pairs)


def table_lookup(table, wanted):
    slot_ids = jnp.arange(table.shape[0], dtype=jnp.int32)
    return jnp.sum(jnp.where(wanted[:, None] == slot_ids[None, :], table[None, :], 0), axis=1)


def double_up(pieces, extra):
    return tuple((jnp.concatenate([mine, theirs], axis=0) for mine, theirs in zip(pieces, extra)))


def reduce_keys(key_sum, value_sum, first_bit):
    for section_bit in reversed(range(key_sum.shape[0].bit_length() - 1)):
        halfway = 1 << section_bit
        far_key, far_value = partner(
            (key_sum[halfway:], value_sum[halfway:]), "ctx", first_bit + section_bit
        )
        key_sum = key_sum[:halfway] + far_key
        value_sum = value_sum[:halfway] + far_value
    return (key_sum[0], value_sum[0])


def per_device(
    queries, key_vectors, value_vectors, attn_output, grad_output, row_logsum, block_place
):
    ctx_count = lax.axis_size("ctx")
    bit_count = ctx_count.bit_length() - 1
    row_bits = (bit_count + 1) // 2
    own_index = lax.axis_index("ctx")
    tokens = queries.shape[0]
    head_size = key_vectors.shape[1]
    head_count = row_logsum.shape[0]
    score_scale = head_size ** (-0.5)
    row_delta = jnp.einsum(
        "thd,thd->ht",
        grad_output.reshape(tokens, head_count, head_size),
        attn_output.reshape(tokens, head_count, head_size),
        preferred_element_type=jnp.float32,
    )
    row_query, row_grad = (queries[None], grad_output[None])
    row_lse_all, row_delta_all = (row_logsum[None], row_delta[None])
    for section_bit in range(row_bits):
        far_query, far_grad = partner((row_query, row_grad), "ctx", section_bit)
        far_lse, far_delta = partner((row_lse_all, row_delta_all), "ctx", section_bit)
        row_query, row_grad = double_up((row_query, row_grad), (far_query, far_grad))
        row_lse_all, row_delta_all = double_up((row_lse_all, row_delta_all), (far_lse, far_delta))
    col_key, col_value = (key_vectors[None], value_vectors[None])
    for section_bit in range(row_bits, bit_count):
        far_key, far_value = partner((col_key, col_value), "ctx", section_bit)
        col_key, col_value = double_up((col_key, col_value), (far_key, far_value))
    row_total = 1 << row_bits
    col_total = 1 << bit_count - row_bits
    pair_width = min(2, col_total)
    group_count = col_total // pair_width
    group_rows = pair_width * tokens
    row_blocks = table_lookup(
        block_place, jnp.bitwise_xor(own_index, jnp.arange(row_total, dtype=jnp.int32))
    )
    col_blocks = table_lookup(
        block_place, jnp.bitwise_xor(own_index, jnp.arange(col_total, dtype=jnp.int32) * row_total)
    )
    offsets = jnp.arange(tokens, dtype=jnp.int32)
    group_place = (col_blocks[:, None] * tokens + offsets[None, :]).reshape(group_count, group_rows)
    group_first = jnp.min(col_blocks.reshape(group_count, pair_width), axis=1)
    key_groups = col_key.reshape(group_count, group_rows, head_size)
    value_groups = col_value.reshape(group_count, group_rows, head_size)
    row_tiles = row_query.reshape(row_total, tokens, head_count, head_size)
    grad_tiles = row_grad.reshape(row_total, tokens, head_count, head_size)

    def row_sweep(key_state, row_index):
        query_tile = row_tiles[row_index]
        grad_tile = grad_tiles[row_index]
        lse_tile = row_lse_all[row_index].T
        delta_tile = row_delta_all[row_index].T
        row_block = row_blocks[row_index]
        row_place = row_block * tokens + offsets

        def group_sweep(tile_state, group_index):

            def visible(state):
                query_acc, key_acc, value_acc = state
                key_tile = key_groups[group_index]
                value_tile = value_groups[group_index]
                col_place = group_place[group_index]
                scores = (
                    jnp.einsum(
                        "thd,kd->thk", query_tile, key_tile, preferred_element_type=jnp.float32
                    )
                    * score_scale
                )
                allowed = col_place[None, None, :] <= row_place[:, None, None]
                attn_prob = jnp.where(allowed, jnp.exp(scores - lse_tile[:, :, None]), 0.0)
                prob_half = attn_prob.astype(jnp.bfloat16)
                grad_prob = jnp.einsum(
                    "thd,kd->thk", grad_tile, value_tile, preferred_element_type=jnp.float32
                )
                grad_score = (attn_prob * (grad_prob - delta_tile[:, :, None])).astype(jnp.bfloat16)
                query_acc = query_acc + jnp.einsum(
                    "thk,kd->thd", grad_score, key_tile, preferred_element_type=jnp.float32
                )
                key_term = jnp.einsum(
                    "thk,thd->kd", grad_score, query_tile, preferred_element_type=jnp.float32
                )
                value_term = jnp.einsum(
                    "thk,thd->kd", prob_half, grad_tile, preferred_element_type=jnp.float32
                )
                key_acc = key_acc.at[group_index].add(key_term)
                value_acc = value_acc.at[group_index].add(value_term)
                return (query_acc, key_acc, value_acc)

            tile_state = lax.cond(
                group_first[group_index] <= row_block, visible, lambda state: state, tile_state
            )
            return (tile_state, None)

        query_zero = jnp.zeros((tokens, head_count, head_size), jnp.float32)
        start_state = (query_zero, key_state[0], key_state[1])
        (query_acc, key_acc, value_acc), unused = lax.scan(
            group_sweep, start_state, jnp.arange(group_count, dtype=jnp.int32)
        )
        return ((key_acc, value_acc), query_acc)

    kv_zero = jnp.zeros((group_count, group_rows, head_size), jnp.float32)
    (key_grouped, value_grouped), query_terms = lax.scan(
        row_sweep, (kv_zero, kv_zero), jnp.arange(row_total, dtype=jnp.int32)
    )
    key_total = key_grouped.reshape(col_total, tokens, head_size)
    value_total = value_grouped.reshape(col_total, tokens, head_size)
    query_sum = query_terms
    for section_bit in reversed(range(row_bits)):
        halfway = 1 << section_bit
        query_sum = query_sum[:halfway] + partner(query_sum[halfway:], "ctx", section_bit)
    grad_queries = (
        (query_sum[0] * score_scale).reshape(tokens, head_count * head_size).astype(jnp.bfloat16)
    )
    key_sum, value_sum = reduce_keys(key_total, value_total, row_bits)
    key_sum, value_sum = lax.psum((key_sum, value_sum), "sub")
    grad_keys = (key_sum * score_scale).astype(jnp.bfloat16)
    grad_values = value_sum.astype(jnp.bfloat16)
    return (grad_queries, grad_keys, grad_values)


MOST_BLOCKS = 16
MESH = pl.DeviceIdType.MESH
HIDE = 1e30


def fused_kernel(
    n, heads,
    q_hbm, k_hbm, v_hbm, o_hbm, g_hbm, l_hbm, b_hbm,
    dq_hbm, dk_hbm, dv_hbm,
    q_v, o_v, g_v, l_v, kv, qt, gt, qs, gs, ds_all, part, sub_in,
    term_out, term_in, fin, dq_v,
    place, load_sem, kv_send, kv_recv, ks_send, ks_recv,
    ps_send, ps_recv, pt_send, pt_recv, fin_sem, out_sem,
):
    nz = n // 2
    tokens, size = k_hbm.shape
    width = heads * tokens
    scale = size ** (-0.5)
    log2e = math.log2(math.e)
    g = lax.axis_index("groups")
    t = lax.axis_index("ctx")
    s = lax.axis_index("sub")
    z, x = t // 2, t % 2
    block = [((z + i // 2) % nz) * 2 + (x + i % 2) % 2 for i in range(n)]
    mirror = [(nz - i // 2) % nz * 2 + i % 2 for i in range(n)]
    near_first = sorted(range(1, n), key=lambda i: (min(i // 2, nz - i // 2), 1 - i % 2))

    loads = [
        pltpu.make_async_copy(k_hbm, kv.at[0, 0], load_sem.at[0]),
        pltpu.make_async_copy(v_hbm, kv.at[0, 1], load_sem.at[1]),
        pltpu.make_async_copy(q_hbm, q_v, load_sem.at[2]),
        pltpu.make_async_copy(g_hbm, g_v, load_sem.at[3]),
        pltpu.make_async_copy(o_hbm, o_v, load_sem.at[4]),
        pltpu.make_async_copy(l_hbm, l_v, load_sem.at[5]),
        pltpu.make_async_copy(b_hbm, place, load_sem.at[6]),
    ]

    peers = [(g, block[i], s) for i in range(1, n)] + [(g, t, 1 - s)]
    barrier = pltpu.get_barrier_semaphore()
    for peer in peers:
        pl.semaphore_signal(barrier, inc=1, device_id=peer, device_id_type=MESH)
    for load in loads:
        load.start()
    loads[0].wait()
    loads[1].wait()
    pl.semaphore_wait(barrier, len(peers))

    def send(source, target, send_sem, recv_sem, device):
        copy = pltpu.make_async_remote_copy(
            src_ref=source, dst_ref=target, send_sem=send_sem, recv_sem=recv_sem,
            device_id=device, device_id_type=MESH,
        )
        copy.start()
        return copy

    came, shared, sent_part, passed = {}, {}, {}, {}
    for i in near_first:
        came[mirror[i]] = send(
            kv.at[0, s], kv.at[mirror[i], s], kv_send.at[i], kv_recv.at[mirror[i]], (g, block[i], s)
        )

    for load in loads[2:]:
        load.wait()
    deltas = []
    for h in range(heads):
        here = slice(h * tokens, (h + 1) * tokens)
        cols = slice(h * size, (h + 1) * size)
        qs[here, :] = q_v[:, cols]
        gs[here, :] = g_v[:, cols]
        qt[:, here] = q_v[:, cols].T
        grad_t = g_v[:, cols].T
        gt[:, here] = grad_t
        out_t = o_v[:, cols].T
        deltas.append(
            jnp.sum(grad_t.astype(jnp.float32) * out_t.astype(jnp.float32), axis=0, keepdims=True)
        )
    delta_row = jnp.concatenate(deltas, axis=1)
    lse_row = jnp.concatenate([l_v[h : h + 1, :] for h in range(heads)], axis=1) * log2e

    own_place = place[t]
    chunk = 2 * tokens if heads % 2 == 0 else tokens

    def score(slot):
        key_tile, value_tile = kv[slot, 0], kv[slot, 1]
        lse = lse_row
        if slot:
            lse = lse + jnp.where(place[block[slot]] < own_place, 0.0, HIDE)
        key_sum = value_sum = None
        for start in range(0, width, chunk):
            here = slice(start, start + chunk)
            scores = jnp.dot(key_tile, qt[:, here], preferred_element_type=jnp.float32)
            grad_prob = jnp.dot(value_tile, gt[:, here], preferred_element_type=jnp.float32)
            prob = jnp.exp2(scores * (scale * log2e) - lse[:, here])
            if slot == 0:
                shape = (tokens, chunk)
                key_place = lax.broadcasted_iota(jnp.int32, shape, 0)
                row_place = lax.broadcasted_iota(jnp.int32, shape, 1) % tokens
                prob = jnp.where(key_place <= row_place, prob, 0.0)
            grad_score = (prob * (grad_prob - delta_row[:, here])).astype(jnp.bfloat16)
            ds_all[slot, :, here] = grad_score
            value_term = jnp.dot(
                prob.astype(jnp.bfloat16), gs[here, :], preferred_element_type=jnp.float32
            )
            key_term = jnp.dot(grad_score, qs[here, :], preferred_element_type=jnp.float32)
            value_sum = value_term if value_sum is None else value_sum + value_term
            key_sum = key_term if key_sum is None else key_sum + key_term
        part[slot, 0] = key_sum
        part[slot, 1] = value_sum
        sent_part[slot] = send(
            part.at[slot, 1 - s], sub_in.at[slot], ps_send.at[slot], ps_recv.at[slot],
            (g, t, 1 - s),
        )

    def pass_on(slot):
        sent_part[slot].wait_recv()
        total = part[slot, s] + sub_in[slot]
        if slot == 0:
            part[slot, s] = total
            return
        term_out[slot] = total.astype(jnp.bfloat16)
        passed[mirror[slot]] = send(
            term_out.at[slot], term_in.at[mirror[slot]], pt_send.at[slot],
            pt_recv.at[mirror[slot]], (g, block[slot], s),
        )

    def share(slot):
        came[slot].wait_recv()
        shared[slot] = send(
            kv.at[slot, s], kv.at[slot, s], ks_send.at[slot], ks_recv.at[slot], (g, t, 1 - s)
        )

    score(0)
    share(near_first[0])
    before = 0
    for i, slot in enumerate(near_first):
        if i + 1 < len(near_first):
            share(near_first[i + 1])
        shared[slot].wait_recv()
        score(slot)
        pass_on(before)
        before = slot
    pass_on(before)
    total = part[0, s]

    keys = kv[:, 0].reshape(n * tokens, size)
    for start in range(0, width, chunk):
        grads = ds_all[:, :, start : start + chunk].reshape(n * tokens, chunk)
        query_t = lax.dot_general(
            keys, grads, (((0,), (0,)), ((), ())), preferred_element_type=jnp.float32
        )
        for first in range(0, chunk, tokens):
            h = (start + first) // tokens
            dq_v[:, h * size : (h + 1) * size] = (
                (query_t[:, first : first + tokens] * scale).T.astype(jnp.bfloat16)
            )
    outs = [pltpu.make_async_copy(dq_v, dq_hbm, out_sem.at[0])]
    outs[0].start()

    for slot in near_first:
        passed[slot].wait_recv()
        total = total + term_in[slot].astype(jnp.float32)
    fin[s] = (total * jnp.where(s == 0, scale, 1.0)).astype(jnp.bfloat16)
    last = send(fin.at[s], fin.at[s], fin_sem.at[0], fin_sem.at[1], (g, t, 1 - s))
    last.wait_recv()
    outs.append(pltpu.make_async_copy(fin.at[0], dk_hbm, out_sem.at[1]))
    outs.append(pltpu.make_async_copy(fin.at[1], dv_hbm, out_sem.at[2]))
    outs[1].start()
    outs[2].start()
    for group in (came, shared, sent_part, passed):
        for copy in group.values():
            copy.wait_send()
    last.wait_send()
    for out in outs:
        out.wait()


def settle_kernel(dq_in, dk_in, dv_in, dq_out, dk_out, dv_out):
    dq_out[...] = dq_in[...]
    dk_out[...] = dk_in[...]
    dv_out[...] = dv_in[...]


def fused_device(
    queries, key_vectors, value_vectors, attn_output, grad_output, row_logsum, block_place
):
    n = lax.axis_size("ctx")
    tokens, size = key_vectors.shape
    heads = row_logsum.shape[0]
    width = heads * tokens
    half, wide = jnp.bfloat16, jnp.float32
    dma = pltpu.SemaphoreType.DMA
    anywhere = pl.BlockSpec(memory_space=pltpu.HBM)
    grads = pl.pallas_call(
        functools.partial(fused_kernel, n, heads),
        out_shape=(
            jax.ShapeDtypeStruct(queries.shape, half),
            jax.ShapeDtypeStruct(key_vectors.shape, half),
            jax.ShapeDtypeStruct(value_vectors.shape, half),
        ),
        in_specs=[anywhere] * 7,
        out_specs=(anywhere,) * 3,
        scratch_shapes=[
            pltpu.VMEM(queries.shape, half),
            pltpu.VMEM(queries.shape, half),
            pltpu.VMEM(queries.shape, half),
            pltpu.VMEM(row_logsum.shape, wide),
            pltpu.VMEM((n, 2, tokens, size), half),
            pltpu.VMEM((size, width), half),
            pltpu.VMEM((size, width), half),
            pltpu.VMEM((width, size), half),
            pltpu.VMEM((width, size), half),
            pltpu.VMEM((n, tokens, width), half),
            pltpu.VMEM((n, 2, tokens, size), wide),
            pltpu.VMEM((n, tokens, size), wide),
            pltpu.VMEM((n, tokens, size), half),
            pltpu.VMEM((n, tokens, size), half),
            pltpu.VMEM((2, tokens, size), half),
            pltpu.VMEM(queries.shape, half),
            pltpu.SMEM(block_place.shape, jnp.int32),
            dma((7,)),
            dma((n,)), dma((n,)),
            dma((n,)), dma((n,)),
            dma((n,)), dma((n,)),
            dma((n,)), dma((n,)),
            dma((2,)),
            dma((3,)),
        ],
        compiler_params=pltpu.CompilerParams(
            collective_id=0, has_side_effects=True, vmem_limit_bytes=60 * 2**20
        ),
        cost_estimate=pl.CostEstimate(
            flops=10 * n * tokens * width * size,
            bytes_accessed=8 * tokens * width,
            transcendentals=n * tokens * width,
        ),
    )(queries, key_vectors, value_vectors, attn_output, grad_output, row_logsum, block_place)
    return pl.pallas_call(
        settle_kernel,
        out_shape=tuple(jax.ShapeDtypeStruct(grad.shape, grad.dtype) for grad in grads),
    )(*grads)


def solution(mesh):
    placed = (
        P(("groups", "ctx"), "sub"),
        P(("groups", "ctx"), None),
        P(("groups", "ctx"), None),
        P(("groups", "ctx"), "sub"),
        P(("groups", "ctx"), "sub"),
        P("sub", ("groups", "ctx")),
        P("groups"),
    )
    ctx_count = mesh.shape["ctx"]
    fused = ctx_count % 2 == 0 and 4 <= ctx_count <= MOST_BLOCKS and mesh.shape["sub"] == 2
    return jax.shard_map(
        fused_device if fused else per_device,
        mesh=mesh,
        in_specs=placed,
        out_specs=(
            P(("groups", "ctx"), "sub"),
            P(("groups", "ctx"), None),
            P(("groups", "ctx"), None),
        ),
        check_vma=False,
    )
```

```python
import functools
import math

import jax
import jax.numpy as jnp
from jax import lax
from jax.experimental import pallas as pl
from jax.experimental.pallas import tpu as pltpu
from jax.sharding import PartitionSpec as P


def partner(value, axis, distance):
    mask = 2**distance
    pairs = [(source, source ^ mask) for source in range(lax.axis_size(axis))]
    return lax.ppermute(value, axis, pairs)


def table_lookup(table, wanted):
    slot_ids = jnp.arange(table.shape[0], dtype=jnp.int32)
    return jnp.sum(jnp.where(wanted[:, None] == slot_ids[None, :], table[None, :], 0), axis=1)


def double_up(pieces, extra):
    return tuple((jnp.concatenate([mine, theirs], axis=0) for mine, theirs in zip(pieces, extra)))


def reduce_keys(key_sum, value_sum, first_bit):
    for section_bit in reversed(range(key_sum.shape[0].bit_length() - 1)):
        halfway = 1 << section_bit
        far_key, far_value = partner(
            (key_sum[halfway:], value_sum[halfway:]), "ctx", first_bit + section_bit
        )
        key_sum = key_sum[:halfway] + far_key
        value_sum = value_sum[:halfway] + far_value
    return (key_sum[0], value_sum[0])


def per_device(
    queries, key_vectors, value_vectors, attn_output, grad_output, row_logsum, block_place
):
    ctx_count = lax.axis_size("ctx")
    bit_count = ctx_count.bit_length() - 1
    row_bits = (bit_count + 1) // 2
    own_index = lax.axis_index("ctx")
    tokens = queries.shape[0]
    head_size = key_vectors.shape[1]
    head_count = row_logsum.shape[0]
    score_scale = head_size ** (-0.5)
    row_delta = jnp.einsum(
        "thd,thd->ht",
        grad_output.reshape(tokens, head_count, head_size),
        attn_output.reshape(tokens, head_count, head_size),
        preferred_element_type=jnp.float32,
    )
    row_query, row_grad = (queries[None], grad_output[None])
    row_lse_all, row_delta_all = (row_logsum[None], row_delta[None])
    for section_bit in range(row_bits):
        far_query, far_grad = partner((row_query, row_grad), "ctx", section_bit)
        far_lse, far_delta = partner((row_lse_all, row_delta_all), "ctx", section_bit)
        row_query, row_grad = double_up((row_query, row_grad), (far_query, far_grad))
        row_lse_all, row_delta_all = double_up((row_lse_all, row_delta_all), (far_lse, far_delta))
    col_key, col_value = (key_vectors[None], value_vectors[None])
    for section_bit in range(row_bits, bit_count):
        far_key, far_value = partner((col_key, col_value), "ctx", section_bit)
        col_key, col_value = double_up((col_key, col_value), (far_key, far_value))
    row_total = 1 << row_bits
    col_total = 1 << bit_count - row_bits
    pair_width = min(2, col_total)
    group_count = col_total // pair_width
    group_rows = pair_width * tokens
    row_blocks = table_lookup(
        block_place, jnp.bitwise_xor(own_index, jnp.arange(row_total, dtype=jnp.int32))
    )
    col_blocks = table_lookup(
        block_place, jnp.bitwise_xor(own_index, jnp.arange(col_total, dtype=jnp.int32) * row_total)
    )
    offsets = jnp.arange(tokens, dtype=jnp.int32)
    group_place = (col_blocks[:, None] * tokens + offsets[None, :]).reshape(group_count, group_rows)
    group_first = jnp.min(col_blocks.reshape(group_count, pair_width), axis=1)
    key_groups = col_key.reshape(group_count, group_rows, head_size)
    value_groups = col_value.reshape(group_count, group_rows, head_size)
    row_tiles = row_query.reshape(row_total, tokens, head_count, head_size)
    grad_tiles = row_grad.reshape(row_total, tokens, head_count, head_size)

    def row_sweep(key_state, row_index):
        query_tile = row_tiles[row_index]
        grad_tile = grad_tiles[row_index]
        lse_tile = row_lse_all[row_index].T
        delta_tile = row_delta_all[row_index].T
        row_block = row_blocks[row_index]
        row_place = row_block * tokens + offsets

        def group_sweep(tile_state, group_index):

            def visible(state):
                query_acc, key_acc, value_acc = state
                key_tile = key_groups[group_index]
                value_tile = value_groups[group_index]
                col_place = group_place[group_index]
                scores = (
                    jnp.einsum(
                        "thd,kd->thk", query_tile, key_tile, preferred_element_type=jnp.float32
                    )
                    * score_scale
                )
                allowed = col_place[None, None, :] <= row_place[:, None, None]
                attn_prob = jnp.where(allowed, jnp.exp(scores - lse_tile[:, :, None]), 0.0)
                prob_half = attn_prob.astype(jnp.bfloat16)
                grad_prob = jnp.einsum(
                    "thd,kd->thk", grad_tile, value_tile, preferred_element_type=jnp.float32
                )
                grad_score = (attn_prob * (grad_prob - delta_tile[:, :, None])).astype(jnp.bfloat16)
                query_acc = query_acc + jnp.einsum(
                    "thk,kd->thd", grad_score, key_tile, preferred_element_type=jnp.float32
                )
                key_term = jnp.einsum(
                    "thk,thd->kd", grad_score, query_tile, preferred_element_type=jnp.float32
                )
                value_term = jnp.einsum(
                    "thk,thd->kd", prob_half, grad_tile, preferred_element_type=jnp.float32
                )
                key_acc = key_acc.at[group_index].add(key_term)
                value_acc = value_acc.at[group_index].add(value_term)
                return (query_acc, key_acc, value_acc)

            tile_state = lax.cond(
                group_first[group_index] <= row_block, visible, lambda state: state, tile_state
            )
            return (tile_state, None)

        query_zero = jnp.zeros((tokens, head_count, head_size), jnp.float32)
        start_state = (query_zero, key_state[0], key_state[1])
        (query_acc, key_acc, value_acc), unused = lax.scan(
            group_sweep, start_state, jnp.arange(group_count, dtype=jnp.int32)
        )
        return ((key_acc, value_acc), query_acc)

    kv_zero = jnp.zeros((group_count, group_rows, head_size), jnp.float32)
    (key_grouped, value_grouped), query_terms = lax.scan(
        row_sweep, (kv_zero, kv_zero), jnp.arange(row_total, dtype=jnp.int32)
    )
    key_total = key_grouped.reshape(col_total, tokens, head_size)
    value_total = value_grouped.reshape(col_total, tokens, head_size)
    query_sum = query_terms
    for section_bit in reversed(range(row_bits)):
        halfway = 1 << section_bit
        query_sum = query_sum[:halfway] + partner(query_sum[halfway:], "ctx", section_bit)
    grad_queries = (
        (query_sum[0] * score_scale).reshape(tokens, head_count * head_size).astype(jnp.bfloat16)
    )
    key_sum, value_sum = reduce_keys(key_total, value_total, row_bits)
    key_sum, value_sum = lax.psum((key_sum, value_sum), "sub")
    grad_keys = (key_sum * score_scale).astype(jnp.bfloat16)
    grad_values = value_sum.astype(jnp.bfloat16)
    return (grad_queries, grad_keys, grad_values)


MOST_BLOCKS = 16
MESH = pl.DeviceIdType.MESH
HIDE = 1e30


def fused_kernel(
    n, heads,
    q_hbm, k_hbm, v_hbm, o_hbm, g_hbm, l_hbm, b_hbm,
    dq_hbm, dk_hbm, dv_hbm,
    q_v, o_v, g_v, l_v, kv, qt, gt, qs, gs, ds_all, part, sub_in,
    term_out, term_in, fin, dq_v,
    place, load_sem, kv_send, kv_recv, ks_send, ks_recv,
    ps_send, ps_recv, pt_send, pt_recv, fin_sem, out_sem,
):
    nz = n // 2
    tokens, size = k_hbm.shape
    width = heads * tokens
    scale = size ** (-0.5)
    log2e = math.log2(math.e)
    g = lax.axis_index("groups")
    t = lax.axis_index("ctx")
    s = lax.axis_index("sub")
    z, x = t // 2, t % 2
    block = [((z + i // 2) % nz) * 2 + (x + i % 2) % 2 for i in range(n)]
    mirror = [(nz - i // 2) % nz * 2 + i % 2 for i in range(n)]
    near_first = sorted(range(1, n), key=lambda i: (min(i // 2, nz - i // 2), 1 - i % 2))

    loads = [
        pltpu.make_async_copy(k_hbm, kv.at[0, 0], load_sem.at[0]),
        pltpu.make_async_copy(v_hbm, kv.at[0, 1], load_sem.at[1]),
        pltpu.make_async_copy(q_hbm, q_v, load_sem.at[2]),
        pltpu.make_async_copy(g_hbm, g_v, load_sem.at[3]),
        pltpu.make_async_copy(o_hbm, o_v, load_sem.at[4]),
        pltpu.make_async_copy(l_hbm, l_v, load_sem.at[5]),
        pltpu.make_async_copy(b_hbm, place, load_sem.at[6]),
    ]

    peers = [(g, block[i], s) for i in range(1, n)] + [(g, t, 1 - s)]
    barrier = pltpu.get_barrier_semaphore()
    for peer in peers:
        pl.semaphore_signal(barrier, inc=1, device_id=peer, device_id_type=MESH)
    for load in loads:
        load.start()

    def send(source, target, send_sem, recv_sem, device):
        copy = pltpu.make_async_remote_copy(
            src_ref=source, dst_ref=target, send_sem=send_sem, recv_sem=recv_sem,
            device_id=device, device_id_type=MESH,
        )
        copy.start()
        return copy

    for load in loads[2:]:
        load.wait()
    deltas = []
    for h in range(heads):
        here = slice(h * tokens, (h + 1) * tokens)
        cols = slice(h * size, (h + 1) * size)
        qs[here, :] = q_v[:, cols]
        gs[here, :] = g_v[:, cols]
        qt[:, here] = q_v[:, cols].T
        grad_t = g_v[:, cols].T
        gt[:, here] = grad_t
        out_t = o_v[:, cols].T
        deltas.append(
            jnp.sum(grad_t.astype(jnp.float32) * out_t.astype(jnp.float32), axis=0, keepdims=True)
        )
    loads[0].wait()
    loads[1].wait()
    pl.semaphore_wait(barrier, len(peers))
    came, shared, sent_part, passed = {}, {}, {}, {}
    for i in near_first:
        came[mirror[i]] = send(
            kv.at[0, s], kv.at[mirror[i], s], kv_send.at[i], kv_recv.at[mirror[i]], (g, block[i], s)
        )

    delta_row = jnp.concatenate(deltas, axis=1)
    lse_row = jnp.concatenate([l_v[h : h + 1, :] for h in range(heads)], axis=1) * log2e

    own_place = place[t]
    chunk = 2 * tokens if heads % 2 == 0 else tokens

    def score(slot):
        key_tile, value_tile = kv[slot, 0], kv[slot, 1]
        lse = lse_row
        if slot:
            lse = lse + jnp.where(place[block[slot]] < own_place, 0.0, HIDE)
        key_sum = value_sum = None
        for start in range(0, width, chunk):
            here = slice(start, start + chunk)
            scores = jnp.dot(key_tile, qt[:, here], preferred_element_type=jnp.float32)
            grad_prob = jnp.dot(value_tile, gt[:, here], preferred_element_type=jnp.float32)
            prob = jnp.exp2(scores * (scale * log2e) - lse[:, here])
            if slot == 0:
                shape = (tokens, chunk)
                key_place = lax.broadcasted_iota(jnp.int32, shape, 0)
                row_place = lax.broadcasted_iota(jnp.int32, shape, 1) % tokens
                prob = jnp.where(key_place <= row_place, prob, 0.0)
            grad_score = (prob * (grad_prob - delta_row[:, here])).astype(jnp.bfloat16)
            ds_all[slot, :, here] = grad_score
            value_term = jnp.dot(
                prob.astype(jnp.bfloat16), gs[here, :], preferred_element_type=jnp.float32
            )
            key_term = jnp.dot(grad_score, qs[here, :], preferred_element_type=jnp.float32)
            value_sum = value_term if value_sum is None else value_sum + value_term
            key_sum = key_term if key_sum is None else key_sum + key_term
        part[slot, 0] = key_sum
        part[slot, 1] = value_sum
        sent_part[slot] = send(
            part.at[slot, 1 - s], sub_in.at[slot], ps_send.at[slot], ps_recv.at[slot],
            (g, t, 1 - s),
        )

    def pass_on(slot):
        sent_part[slot].wait_recv()
        total = part[slot, s] + sub_in[slot]
        if slot == 0:
            part[slot, s] = total
            return
        term_out[slot] = total.astype(jnp.bfloat16)
        passed[mirror[slot]] = send(
            term_out.at[slot], term_in.at[mirror[slot]], pt_send.at[slot],
            pt_recv.at[mirror[slot]], (g, block[slot], s),
        )

    def share(slot):
        came[slot].wait_recv()
        shared[slot] = send(
            kv.at[slot, s], kv.at[slot, s], ks_send.at[slot], ks_recv.at[slot], (g, t, 1 - s)
        )

    score(0)
    share(near_first[0])
    before = 0
    for i, slot in enumerate(near_first):
        if i + 1 < len(near_first):
            share(near_first[i + 1])
        shared[slot].wait_recv()
        score(slot)
        pass_on(before)
        before = slot
    pass_on(before)
    total = part[0, s]

    keys = kv[:, 0].reshape(n * tokens, size)
    for start in range(0, width, chunk):
        grads = ds_all[:, :, start : start + chunk].reshape(n * tokens, chunk)
        query_t = lax.dot_general(
            keys, grads, (((0,), (0,)), ((), ())), preferred_element_type=jnp.float32
        )
        for first in range(0, chunk, tokens):
            h = (start + first) // tokens
            dq_v[:, h * size : (h + 1) * size] = (
                (query_t[:, first : first + tokens] * scale).T.astype(jnp.bfloat16)
            )
    outs = [pltpu.make_async_copy(dq_v, dq_hbm, out_sem.at[0])]
    outs[0].start()

    for slot in near_first:
        passed[slot].wait_recv()
        total = total + term_in[slot].astype(jnp.float32)
    fin[s] = (total * jnp.where(s == 0, scale, 1.0)).astype(jnp.bfloat16)
    last = send(fin.at[s], fin.at[s], fin_sem.at[0], fin_sem.at[1], (g, t, 1 - s))
    last.wait_recv()
    outs.append(pltpu.make_async_copy(fin.at[0], dk_hbm, out_sem.at[1]))
    outs.append(pltpu.make_async_copy(fin.at[1], dv_hbm, out_sem.at[2]))
    outs[1].start()
    outs[2].start()
    for group in (came, shared, sent_part, passed):
        for copy in group.values():
            copy.wait_send()
    last.wait_send()
    for out in outs:
        out.wait()


def settle_kernel(dq_in, dk_in, dv_in, dq_out, dk_out, dv_out):
    dq_out[...] = dq_in[...]
    dk_out[...] = dk_in[...]
    dv_out[...] = dv_in[...]


def fused_device(
    queries, key_vectors, value_vectors, attn_output, grad_output, row_logsum, block_place
):
    n = lax.axis_size("ctx")
    tokens, size = key_vectors.shape
    heads = row_logsum.shape[0]
    width = heads * tokens
    half, wide = jnp.bfloat16, jnp.float32
    dma = pltpu.SemaphoreType.DMA
    anywhere = pl.BlockSpec(memory_space=pltpu.HBM)
    grads = pl.pallas_call(
        functools.partial(fused_kernel, n, heads),
        out_shape=(
            jax.ShapeDtypeStruct(queries.shape, half),
            jax.ShapeDtypeStruct(key_vectors.shape, half),
            jax.ShapeDtypeStruct(value_vectors.shape, half),
        ),
        in_specs=[anywhere] * 7,
        out_specs=(anywhere,) * 3,
        scratch_shapes=[
            pltpu.VMEM(queries.shape, half),
            pltpu.VMEM(queries.shape, half),
            pltpu.VMEM(queries.shape, half),
            pltpu.VMEM(row_logsum.shape, wide),
            pltpu.VMEM((n, 2, tokens, size), half),
            pltpu.VMEM((size, width), half),
            pltpu.VMEM((size, width), half),
            pltpu.VMEM((width, size), half),
            pltpu.VMEM((width, size), half),
            pltpu.VMEM((n, tokens, width), half),
            pltpu.VMEM((n, 2, tokens, size), wide),
            pltpu.VMEM((n, tokens, size), wide),
            pltpu.VMEM((n, tokens, size), half),
            pltpu.VMEM((n, tokens, size), half),
            pltpu.VMEM((2, tokens, size), half),
            pltpu.VMEM(queries.shape, half),
            pltpu.SMEM(block_place.shape, jnp.int32),
            dma((7,)),
            dma((n,)), dma((n,)),
            dma((n,)), dma((n,)),
            dma((n,)), dma((n,)),
            dma((n,)), dma((n,)),
            dma((2,)),
            dma((3,)),
        ],
        compiler_params=pltpu.CompilerParams(
            collective_id=0, has_side_effects=True, vmem_limit_bytes=60 * 2**20
        ),
        cost_estimate=pl.CostEstimate(
            flops=10 * n * tokens * width * size,
            bytes_accessed=8 * tokens * width,
            transcendentals=n * tokens * width,
        ),
    )(queries, key_vectors, value_vectors, attn_output, grad_output, row_logsum, block_place)
    return pl.pallas_call(
        settle_kernel,
        out_shape=tuple(jax.ShapeDtypeStruct(grad.shape, grad.dtype) for grad in grads),
    )(*grads)


def solution(mesh):
    placed = (
        P(("groups", "ctx"), "sub"),
        P(("groups", "ctx"), None),
        P(("groups", "ctx"), None),
        P(("groups", "ctx"), "sub"),
        P(("groups", "ctx"), "sub"),
        P("sub", ("groups", "ctx")),
        P("groups"),
    )
    ctx_count = mesh.shape["ctx"]
    fused = ctx_count % 2 == 0 and 4 <= ctx_count <= MOST_BLOCKS and mesh.shape["sub"] == 2
    return jax.shard_map(
        fused_device if fused else per_device,
        mesh=mesh,
        in_specs=placed,
        out_specs=(
            P(("groups", "ctx"), "sub"),
            P(("groups", "ctx"), None),
            P(("groups", "ctx"), None),
        ),
        check_vma=False,
    )
```
